512 devices in a mesh: dp: 32 (over x, z_hi, y), expert: 16 (over z_lo, core).
Axes of the slice: x: 4, y: 4, z: 16 (z_hi: 2, z_lo: 8; z = z_hi * 8 + z_lo), core: 2. Of those that a mesh axis runs over, the one named last changes fastest.
Arguments:
- tokens: bfloat16 [65536, 1280], P(('dp', 'expert')), may hold values from -12 to 12
- out_grad: bfloat16 [65536, 1280], P(('dp', 'expert')), may hold values from -6 to 6
- slot_param: bfloat16 [1280, 128], replicated, may hold values from -1 to 1
- w_in: bfloat16 [512, 640, 1280], P(('dp', 'expert')), may hold values from -0.15625 to 0.15625
- w_out: bfloat16 [512, 640, 1280], P(('dp', 'expert')), may hold values from -0.125 to 0.125
Outputs:
- token_grad: bfloat16 [65536, 1280], P(('dp', 'expert'))
- param_grad: bfloat16 [1280, 128], P('dp', 'expert')
The draws below stay inside these ranges and needn't reach their ends.
All inputs are finite; a program needn't handle non-finite values.
Results may differ from the reference program's by a relative error of at most 0.018.
Values may be sent and summed in bfloat16 or wider, within the bound.
A program may use at most 64 MiB of HBM per device.

```python
import math
import jax
import jax.numpy as jnp
from jax import lax

D = 1280
FFN = 2560
IMAGE = 256
EXPERTS = 128
TOKENS = 65536
IMAGES = 256


def draw_tokens(key, part):
    key = jax.random.fold_in(key, 11)
    first_key, second_key = jax.random.split(key)
    base_draw = jnp.clip(jax.random.normal(first_key, (TOKENS, D), jnp.float32), -4.0, 4.0)
    scales = jnp.exp(jax.random.uniform(second_key, (TOKENS, 1), jnp.float32, math.log(0.3), math.log(3.0)))
    result = base_draw * scales
    return result.astype(jnp.bfloat16)


def draw_slot_param(key, part):
    key = jax.random.fold_in(key, 23)
    first_key, second_key = jax.random.split(key)
    base_draw = jnp.clip(jax.random.normal(first_key, (D, EXPERTS), jnp.float32), -4.0, 4.0)
    scales = jnp.exp(jax.random.uniform(second_key, (1, EXPERTS), jnp.float32, math.log(0.4), math.log(1.6)))
    result = base_draw * scales / math.sqrt(D)
    return result.astype(jnp.bfloat16)


def block_scale(key, extent, cuts, low, top_value):
    level = 1.0
    for axis_at, blocks in cuts:
        heights = jax.random.uniform(jax.random.fold_in(jax.random.fold_in(key, 6), axis_at), (blocks,), jnp.float32, low / len(cuts), top_value / len(cuts))
        level = level * jnp.repeat(jnp.exp(heights), extent[axis_at] // blocks).reshape((-1,) + (1,) * (len(extent) - 1 - axis_at))
    return level


def noise(stream_key, shape, width, limit, cuts=(), kind=jnp.bfloat16):
    entries = jax.random.normal(stream_key, shape, jnp.float32) * width
    if len(cuts) > 0:
        entries = block_scale(stream_key, shape, cuts, -0.22, 0.18) * entries
    return jnp.clip(entries, min=-limit, max=limit).astype(kind)


def setup_inputs(seed: int = 0) -> dict:
    splits = jax.random.split(jax.random.key(seed), 6)
    return {
        "tokens": draw_tokens(jax.random.fold_in(splits[5], 71), 0),
        "out_grad": noise(splits[1], (TOKENS, D), 1.0, 6.0, ((0, 512),)),
        "slot_param": draw_slot_param(jax.random.fold_in(splits[5], 71), 0),
        "w_in": noise(splits[3], (EXPERTS * 4, FFN // 4, D), D ** -0.5, 0.15625, ((0, 512),)),
        "w_out": noise(splits[4], (EXPERTS * 4, FFN // 4, D), FFN ** -0.5, 0.125, ((0, 512),)),
    }


gelu_scale = 0.7978845608
gelu_cubic = 0.044715


def gelu_parts(pre_act):
    inner_arg = gelu_scale * (pre_act + gelu_cubic * pre_act * pre_act * pre_act)
    tangent = jnp.tanh(inner_arg)
    gelu_value = 0.5 * pre_act * (1.0 + tangent)
    gelu_slope = 0.5 * (1.0 + tangent) + 0.5 * pre_act * (1.0 - tangent * tangent) * gelu_scale * (1.0 + 3.0 * gelu_cubic * pre_act * pre_act)
    return gelu_value, gelu_slope


def reference(tokens, out_grad, slot_param, w_in, w_out):
    highest = lax.Precision.HIGHEST
    logits = jnp.dot(tokens, slot_param, preferred_element_type=jnp.float32)
    grouped = logits.reshape(IMAGES, IMAGE, EXPERTS)
    col_exp = jnp.exp(grouped - jnp.max(grouped, axis=1, keepdims=True))
    dispatch = (col_exp / jnp.sum(col_exp, axis=1, keepdims=True)).reshape(TOKENS, EXPERTS)
    row_exp = jnp.exp(logits - jnp.max(logits, axis=1, keepdims=True))
    combine = row_exp / jnp.sum(row_exp, axis=1, keepdims=True)
    dispatch_b = dispatch.astype(jnp.bfloat16)
    combine_b = combine.astype(jnp.bfloat16)
    tokens_f = tokens.astype(jnp.float32).reshape(IMAGES, IMAGE, D)
    grads_f = out_grad.astype(jnp.float32).reshape(IMAGES, IMAGE, D)
    disp_f = dispatch_b.astype(jnp.float32).reshape(IMAGES, IMAGE, EXPERTS)
    comb_f = combine_b.astype(jnp.float32).reshape(IMAGES, IMAGE, EXPERTS)
    slot_in = jnp.einsum('nte,ntd->end', disp_f, tokens_f, precision=highest).astype(jnp.bfloat16)
    slot_grad = jnp.einsum('nte,ntd->end', comb_f, grads_f, precision=highest).astype(jnp.bfloat16)
    first_all = w_in.reshape(EXPERTS, FFN, D)
    second_all = w_out.reshape(EXPERTS, FFN, D)

    def expert_step(inputs):
        rows_in, rows_grad, first, second = inputs
        first_f = first.astype(jnp.float32)
        second_f = second.astype(jnp.float32)
        pre_act = jnp.dot(rows_in.astype(jnp.float32), first_f.T, precision=highest)
        gelu_value, gelu_slope = gelu_parts(pre_act)
        slot_out_e = jnp.dot(gelu_value.astype(jnp.bfloat16).astype(jnp.float32), second_f, precision=highest).astype(jnp.bfloat16)
        hidden_grad = jnp.dot(rows_grad.astype(jnp.float32), second_f.T, precision=highest)
        pre_grad = (hidden_grad * gelu_slope).astype(jnp.bfloat16)
        in_grad_e = jnp.dot(pre_grad.astype(jnp.float32), first_f, precision=highest).astype(jnp.bfloat16)
        return slot_out_e, in_grad_e

    slot_out, slot_in_grad = lax.map(expert_step, (slot_in, slot_grad, first_all, second_all))
    comb_grad = jnp.einsum('ntd,end->nte', grads_f, slot_out.astype(jnp.float32), precision=highest)
    disp_grad = jnp.einsum('ntd,end->nte', tokens_f, slot_in_grad.astype(jnp.float32), precision=highest)
    combine3 = combine.reshape(IMAGES, IMAGE, EXPERTS)
    dispatch3 = dispatch.reshape(IMAGES, IMAGE, EXPERTS)
    comb_inner = jnp.sum(combine3 * comb_grad, axis=2, keepdims=True)
    disp_inner = jnp.sum(dispatch3 * disp_grad, axis=1, keepdims=True)
    logit_grad = (combine3 * (comb_grad - comb_inner) + dispatch3 * (disp_grad - disp_inner)).reshape(TOKENS, EXPERTS).astype(jnp.bfloat16)
    mixed = jnp.einsum('nte,end->ntd', disp_f, slot_in_grad.astype(jnp.float32), precision=highest).reshape(TOKENS, D)
    token_grad = (mixed + jnp.dot(logit_grad, slot_param.T, preferred_element_type=jnp.float32)).astype(jnp.bfloat16)
    param_grad = jnp.dot(tokens.T, logit_grad, preferred_element_type=jnp.float32).astype(jnp.bfloat16)
    return token_grad, param_grad
```

```python
import jax
import jax.numpy as jnp
from jax import lax
from jax.sharding import PartitionSpec as P

gelu_scale = 0.7978845608
gelu_cubic = 0.044715


def from_partner(block, axis, stride):
    count = lax.axis_size(axis)
    route = []
    for low in range(count):
        high = low | 1 << stride
        if high != low and high < count:
            route += [(low, high), (high, low)]
    return lax.ppermute(block, axis, route)


def gelu_parts(pre_act):
    inner_arg = gelu_scale * (pre_act + gelu_cubic * pre_act * pre_act * pre_act)
    tangent = jnp.tanh(inner_arg)
    gelu_value = 0.5 * pre_act * (1.0 + tangent)
    gelu_slope = 0.5 * (1.0 + tangent) + 0.5 * pre_act * (1.0 - tangent * tangent) * gelu_scale * (
        1.0 + 3.0 * gelu_cubic * pre_act * pre_act
    )
    return (gelu_value, gelu_slope)


def shards(tokens, out_grad, slot_param, w_in, w_out):
    ranks = lax.axis_size("dp")
    ranks_ex = lax.axis_size("expert")
    experts = slot_param.shape[1]
    width = tokens.shape[1]
    quarter = width // 4
    images = ranks * ranks_ex // 2
    position = lax.axis_index("expert")
    logits = jnp.dot(tokens, slot_param, preferred_element_type=jnp.float32)
    local_max = jnp.max(logits, axis=0)
    col_max = jnp.maximum(local_max, from_partner(local_max, "expert", 0))
    half_sum = jnp.sum(jnp.exp(logits - col_max), axis=0)
    col_sum = half_sum + from_partner(half_sum, "expert", 0)
    dispatch = jnp.exp(logits - col_max) / col_sum
    row_exp = jnp.exp(logits - jnp.max(logits, axis=1, keepdims=True))
    combine = row_exp / jnp.sum(row_exp, axis=1, keepdims=True)
    dispatch_b = dispatch.astype(jnp.bfloat16)
    combine_b = combine.astype(jnp.bfloat16)
    slot_in_part = jnp.einsum("te,td->ed", dispatch_b, tokens, preferred_element_type=jnp.float32)
    slot_grad_part = jnp.einsum(
        "te,td->ed", combine_b, out_grad, preferred_element_type=jnp.float32
    )
    in_blocks = slot_in_part.reshape(ranks, ranks_ex, quarter)
    grad_blocks = slot_grad_part.reshape(ranks, ranks_ex, quarter)
    recv_in, recv_grad = (
        lax.all_to_all(
            lax.all_to_all(in_blocks, "dp", split_axis=0, concat_axis=0, tiled=True),
            "expert",
            split_axis=1,
            concat_axis=1,
            tiled=True,
        ),
        lax.all_to_all(
            lax.all_to_all(grad_blocks, "dp", split_axis=0, concat_axis=0, tiled=True),
            "expert",
            split_axis=1,
            concat_axis=1,
            tiled=True,
        ),
    )
    slot_in_cols = (
        jnp.sum(recv_in.reshape(ranks, ranks_ex // 2, 2, quarter), axis=2)
        .reshape(images, quarter)
        .astype(jnp.bfloat16)
    )
    slot_grad_cols = (
        jnp.sum(recv_grad.reshape(ranks, ranks_ex // 2, 2, quarter), axis=2)
        .reshape(images, quarter)
        .astype(jnp.bfloat16)
    )
    whole_in = slot_in_cols
    whole_grad = slot_grad_cols
    for bit in range(2):
        other_in, other_grad = from_partner((whole_in, whole_grad), "expert", bit)
        upper = position // (1 << bit) % 2 == 1
        whole_in = jnp.where(
            upper,
            jnp.concatenate([other_in, whole_in], 1),
            jnp.concatenate([whole_in, other_in], 1),
        )
        whole_grad = jnp.where(
            upper,
            jnp.concatenate([other_grad, whole_grad], 1),
            jnp.concatenate([whole_grad, other_grad], 1),
        )
    first = w_in[0]
    second = w_out[0]
    pre_act = jnp.einsum("nd,fd->nf", whole_in, first, preferred_element_type=jnp.float32)
    gelu_value, gelu_slope = gelu_parts(pre_act)
    out_part = jnp.dot(gelu_value.astype(jnp.bfloat16), second, preferred_element_type=jnp.float32)
    hidden_grad = jnp.einsum("nd,fd->nf", whole_grad, second, preferred_element_type=jnp.float32)
    pre_grad = (hidden_grad * gelu_slope).astype(jnp.bfloat16)
    back_part = jnp.dot(pre_grad, first, preferred_element_type=jnp.float32)
    for bit in (1, 0):
        span = out_part.shape[1] // 2
        upper = position // (1 << bit) % 2 == 1
        keep_out = jnp.where(upper, out_part[:, span:], out_part[:, :span])
        give_out = jnp.where(upper, out_part[:, :span], out_part[:, span:])
        keep_back = jnp.where(upper, back_part[:, span:], back_part[:, :span])
        give_back = jnp.where(upper, back_part[:, :span], back_part[:, span:])
        got_out, got_back = from_partner((give_out, give_back), "expert", bit)
        out_part = keep_out + got_out
        back_part = keep_back + got_back

    def spread(rows):
        blocks = rows.astype(jnp.bfloat16).reshape(ranks, ranks_ex // 2, 1, quarter)
        return jnp.broadcast_to(blocks, (ranks, ranks_ex // 2, 2, quarter)).reshape(
            ranks, ranks_ex, quarter
        )

    back_out, back_in = (
        lax.all_to_all(
            lax.all_to_all(spread(out_part), "dp", split_axis=0, concat_axis=0, tiled=True),
            "expert",
            split_axis=1,
            concat_axis=1,
            tiled=True,
        ),
        lax.all_to_all(
            lax.all_to_all(spread(back_part), "dp", split_axis=0, concat_axis=0, tiled=True),
            "expert",
            split_axis=1,
            concat_axis=1,
            tiled=True,
        ),
    )
    slot_out = back_out.reshape(experts, width)
    slot_in_grad = back_in.reshape(experts, width)
    comb_grad = jnp.einsum("td,ed->te", out_grad, slot_out, preferred_element_type=jnp.float32)
    disp_grad = jnp.einsum("td,ed->te", tokens, slot_in_grad, preferred_element_type=jnp.float32)
    disp_local = jnp.sum(dispatch * disp_grad, axis=0)
    disp_inner = disp_local + from_partner(disp_local, "expert", 0)
    comb_inner = jnp.sum(combine * comb_grad, axis=1, keepdims=True)
    logit_grad = (combine * (comb_grad - comb_inner) + dispatch * (disp_grad - disp_inner)).astype(
        jnp.bfloat16
    )
    token_grad = (
        jnp.dot(dispatch_b, slot_in_grad, preferred_element_type=jnp.float32)
        + jnp.einsum("te,de->td", logit_grad, slot_param, preferred_element_type=jnp.float32)
    ).astype(jnp.bfloat16)
    param_part = jnp.einsum("td,te->de", tokens, logit_grad, preferred_element_type=jnp.float32)
    param_rows = jnp.sum(
        lax.all_to_all(
            param_part.reshape(ranks, width // ranks, experts),
            "dp",
            split_axis=0,
            concat_axis=0,
            tiled=True,
        ),
        axis=0,
    )
    param_cols = param_rows.reshape(width // ranks, ranks_ex, experts // ranks_ex)
    param_grad = jnp.sum(
        lax.all_to_all(
            param_cols.transpose(1, 0, 2), "expert", split_axis=0, concat_axis=0, tiled=True
        ),
        axis=0,
    ).astype(jnp.bfloat16)
    return (token_grad, param_grad)


def solution(mesh):
    placed = (
        P(("dp", "expert"), None),
        P(("dp", "expert"), None),
        P(),
        P(("dp", "expert"), None, None),
        P(("dp", "expert"), None, None),
    )
    return jax.shard_map(
        shards,
        mesh=mesh,
        in_specs=placed,
        out_specs=(P(("dp", "expert"), None), P("dp", "expert")),
        check_vma=False,
    )
```

```python
import functools

import jax
import jax.numpy as jnp
from jax import lax
from jax.experimental import pallas as pl
from jax.experimental.pallas import tpu as pltpu
from jax.sharding import PartitionSpec as P

MESH = pl.DeviceIdType.MESH
PLANE_Y = 4

gelu_scale = 0.7978845608
gelu_cubic = 0.044715

F32 = jnp.float32
BF16 = jnp.bfloat16


def gelu_parts(pre_act):
    inner_arg = gelu_scale * (pre_act + gelu_cubic * pre_act * pre_act * pre_act)
    tangent = jnp.tanh(inner_arg)
    gelu_value = 0.5 * pre_act * (1.0 + tangent)
    gelu_slope = 0.5 * (1.0 + tangent) + 0.5 * pre_act * (1.0 - tangent * tangent) * gelu_scale * (
        1.0 + 3.0 * gelu_cubic * pre_act * pre_act
    )
    return (gelu_value, gelu_slope)


def dot(a, b, ca, cb):
    return lax.dot_general(a, b, (((ca,), (cb,)), ((), ())), preferred_element_type=F32)


def tiles(extent, step=256):
    return [(at, min(step, extent - at)) for at in range(0, extent, step)]


def log2(n):
    return n.bit_length() - 1


def kernel(
    nx, ny, zl_n,
    tok_hbm, og_hbm, sp_hbm, w1_hbm, w2_hbm,
    tg_ref, pg_ref,
    tok, og, sp, w1, w2, spt, tokt, disp, comb, disp_b, lg_b,
    s_buf, r_buf, t_buf, x_buf, gv, pgd, p_buf, o_send, o_recv, u_buf, v_buf, q_buf, b_buf, c_buf, g_buf,
    pg_send, pg_recv, pad, f2_send, f2_recv,
    load_sem, swap_s, swap_r, p1_s, p1_r, p2_s, p2_r, rl_s, dd_s, dd_r, o_s, o_r,
    v_s, v_r, b_s, b_r, g_s, g_r, gd_s, gd_r, f1_s, f1_r, f2_s, f2_r,
):
    plane, ring, pairs = nx * ny, 2 * zl_n, zl_n
    at_dp, at_ex = lax.axis_index("dp"), lax.axis_index("expert")
    core, zl = lax.rem(at_ex, 2), lax.div(at_ex, 2)
    y, xz = lax.rem(at_dp, ny), lax.div(at_dp, ny)
    zh, x = lax.rem(xz, 2), lax.div(xz, 2)
    z, xy = zh * zl_n + zl, x * ny + y
    sign = 2 * lax.rem(z, 2) - 1
    pair = lax.div(z, 2)
    other = 1 - core

    def turn(v):
        return lax.rem(v + 2 * ring, ring)

    def shift(j):
        return lax.rem(xy + j, plane)

    def device(xy_to, z_to, core_to):
        x_to, y_to = lax.div(xy_to, ny), lax.rem(xy_to, ny)
        return (
            (x_to * 2 + lax.div(z_to, zl_n)) * ny + y_to,
            lax.rem(z_to, zl_n) * 2 + core_to,
        )

    partner = device(xy, z, other)
    sibling_z = turn(z - sign)
    sibling = device(xy, sibling_z, core)
    started = []

    def send(src, dst, send_sem, recv_sem, to):
        copy = pltpu.make_async_remote_copy(
            src_ref=src, dst_ref=dst, send_sem=send_sem, recv_sem=recv_sem,
            device_id=to, device_id_type=MESH,
        )
        copy.start()
        started.append(copy)

    def arrived(dst, recv_sem):
        pltpu.make_async_remote_copy(
            src_ref=dst, dst_ref=dst, send_sem=recv_sem, recv_sem=recv_sem,
            device_id=partner, device_id_type=MESH,
        ).wait_recv()

    rows, width = tok_hbm.shape
    half = width // 2
    image = 2 * rows
    slots = plane * pairs
    own_cols = pl.ds(pl.multiple_of(core * half, half), half)

    barrier = pltpu.get_barrier_semaphore()
    pl.semaphore_signal(barrier, inc=1, device_id=partner, device_id_type=MESH)
    for j in range(1, plane):
        pl.semaphore_signal(barrier, inc=1, device_id=device(shift(j), z, core), device_id_type=MESH)
    for j in range(1, ring):
        for to in range(2):
            pl.semaphore_signal(
                barrier, inc=1, device_id=device(xy, turn(z + j), to), device_id_type=MESH
            )

    loads = [
        pltpu.make_async_copy(src, dst, load_sem.at[i])
        for i, (src, dst) in enumerate(
            [(tok_hbm, tok.at[core]), (og_hbm, og.at[core]), (sp_hbm, sp), (w1_hbm.at[0], w1), (w2_hbm.at[0], w2)]
        )
    ]
    for load in loads:
        load.start()

    place = lax.broadcasted_iota(jnp.int32, (slots, slots), 0)
    zl2_n = pairs // 2
    of_place = (
        (place >> log2(pairs * ny)) * (2 * ny * zl2_n)
        + ((place >> log2(zl2_n)) & 1) * (ny * zl2_n)
        + ((place >> log2(pairs)) & (ny - 1)) * zl2_n
        + (place & (zl2_n - 1))
    )
    slot_order = (lax.broadcasted_iota(jnp.int32, (slots, slots), 1) == of_place).astype(F32).astype(BF16)
    loads[2].wait()
    spt[...] = dot(slot_order, sp[...], 1, 1).astype(BF16)
    loads[0].wait()
    loads[1].wait()

    pl.semaphore_wait(barrier, plane + 2 * (ring - 1))
    send(tok.at[core], tok.at[core], swap_s.at[0], swap_r.at[0], partner)
    send(og.at[core], og.at[core], swap_s.at[1], swap_r.at[1], partner)
    arrived(tok.at[other], swap_r.at[0])

    tok_all = tok[...].reshape(image, width)
    logits = dot(spt[...], tok_all, 1, 1)
    col_exp = jnp.exp(logits - jnp.max(logits, axis=1, keepdims=True))
    dispatch = col_exp / jnp.sum(col_exp, axis=1, keepdims=True)
    row_exp = jnp.exp(logits - jnp.max(logits, axis=0, keepdims=True))
    combine = row_exp / jnp.sum(row_exp, axis=0, keepdims=True)
    disp[...] = dispatch
    comb[...] = combine
    disp_b[...] = dispatch.astype(BF16)
    slot_in = dot(dispatch.astype(BF16), tok[:, :, own_cols].reshape(image, half), 1, 0)
    arrived(og.at[other], swap_r.at[1])
    slot_grad = dot(combine.astype(BF16), og[:, :, own_cols].reshape(image, half), 1, 0)
    s_buf[...] = jnp.concatenate(
        [slot_in.reshape(plane, pairs, half), slot_grad.reshape(plane, pairs, half)], axis=1
    ).astype(BF16)

    for j in range(1, plane):
        to = shift(j)
        send(s_buf.at[to], r_buf.at[xy], p1_s.at[j], p1_r.at[xy], device(to, z, core))
    r_buf[xy] = s_buf[xy]

    cells = 2 * pairs * plane
    first_at = lax.broadcasted_iota(jnp.int32, (cells, cells), 0)
    second_at = lax.broadcasted_iota(jnp.int32, (cells, cells), 1)

    def by_source(at):
        source = at & (plane - 1)
        kind = (at >> log2(plane)) & 1
        return source * (2 * pairs) + kind * pairs + (at >> log2(2 * plane))

    to_pairs = (second_at == by_source(first_at)).astype(F32).astype(BF16)
    to_sources = (first_at == by_source(second_at)).astype(F32).astype(BF16)

    for j in range(1, plane):
        arrived(r_buf.at[shift(j)], p1_r.at[shift(j)])
    t_buf[...] = dot(to_pairs, r_buf[...].reshape(cells, half), 1, 0).astype(BF16).reshape(
        pairs, 2, plane, half
    )

    here = x_buf.at[core, :, z]
    reach = pairs - 1
    hops = [(sign, d) for d in range(1, pairs, 2)] + [(-sign, d) for d in range(2, pairs, 2)]
    hops.sort(key=lambda hop: hop[1])
    for j, (way, d) in enumerate(hops):
        to = turn(z + way * d)
        send(t_buf.at[lax.div(to, 2)], here, p2_s.at[j], p2_r.at[z], device(xy, to, core))
    send(t_buf.at[pair], here, p2_s.at[reach], p2_r.at[z], sibling)
    send(t_buf.at[pair], here, dd_s.at[z], dd_r.at[z], partner)
    x_buf[core, :, z] = t_buf[pair]

    for at, n in tiles(width, 128):
        tokt[at : at + n] = tok[:, :, at : at + n].reshape(image, n).astype(F32).T.astype(BF16)

    def take(src):
        arrived(x_buf.at[core, :, src], p2_r.at[src])
        send(x_buf.at[core, :, src], x_buf.at[core, :, src], dd_s.at[src], dd_r.at[src], partner)

    for j in range(1, reach + 1):
        src = turn(z + sign * j)
        take(src)
        slot = x_buf.at[core, :, src]
        send(slot, slot, rl_s.at[j], p2_r.at[src], sibling)
        take(turn(z - sign * j))
    take(turn(z - sign * pairs))
    for j in range(ring):
        src = turn(z + j)
        arrived(x_buf.at[other, :, src], dd_r.at[src])

    loads[3].wait()
    loads[4].wait()
    images = ring * plane
    hidden = w1.shape[0]

    def both(kind, weights, at, n):
        return sum(
            dot(x_buf[h, kind].reshape(images, half), weights[at : at + n, h * half : (h + 1) * half], 1, 1)
            for h in range(2)
        )

    for at, n in tiles(hidden):
        gelu_value, gelu_slope = gelu_parts(both(0, w1, at, n))
        gv[:, at : at + n] = gelu_value.astype(BF16)
        pgd[:, at : at + n] = (both(1, w2, at, n) * gelu_slope).astype(BF16)

    def product(kind, whose, at, n):
        left, right = ((gv, w2), (pgd, w1))[kind]
        cols = pl.ds(pl.multiple_of(whose * half + at, 128), n)
        return dot(left[...], right[:, cols], 1, 0).reshape(ring, plane, n)

    for kind in range(2):
        for at, n in tiles(half):
            o_send[kind, :, :, at : at + n] = product(kind, other, at, n).astype(BF16)
        send(o_send.at[kind], o_recv.at[kind], o_s.at[kind], o_r.at[kind], partner)
    for kind in range(2):
        for at, n in tiles(half):
            p_buf[kind, :, :, at : at + n] = product(kind, core, at, n)
    for kind in range(2):
        arrived(o_recv.at[kind], o_r.at[kind])
        p_buf[kind] = p_buf[kind] + o_recv[kind].astype(F32)
        u_buf[kind] = p_buf[kind].astype(BF16)

    for j in range(1, pairs + 1):
        to = turn(z - sign * (pairs + 1 - j))
        send(u_buf.at[:, to], v_buf.at[:, to], v_s.at[j - 1], v_r.at[to], sibling)
    for j in range(reach, 0, -1):
        to = turn(z + sign * j)
        arrived(v_buf.at[:, to], v_r.at[to])
        q_buf[j - 1] = (p_buf[:, to] + v_buf[:, to].astype(F32)).astype(BF16)
        send(q_buf.at[j - 1], b_buf.at[pair], b_s.at[j - 1], b_r.at[pair], device(xy, to, core))
    arrived(v_buf.at[:, z], v_r.at[z])
    b_buf[pair] = (p_buf[:, z] + v_buf[:, z].astype(F32)).astype(BF16)
    for j in range(1, pairs):
        src = lax.rem(pair + j, pairs)
        arrived(b_buf.at[src], b_r.at[src])
    c_buf[...] = dot(to_sources, b_buf[...].reshape(cells, half), 1, 0).astype(BF16).reshape(
        plane, 2 * pairs, half
    )

    def hand_over(src):
        slot = g_buf.at[core, src]
        send(slot, slot, gd_s.at[src], gd_r.at[src], partner)

    for j in range(1, plane):
        to = shift(j)
        send(c_buf.at[to], g_buf.at[core, xy], g_s.at[j], g_r.at[xy], device(to, z, core))
    g_buf[core, xy] = c_buf[xy]
    hand_over(xy)
    for j in range(1, plane):
        src = shift(plane - j)
        arrived(g_buf.at[core, src], g_r.at[src])
        hand_over(src)
    for j in range(plane):
        src = shift(j)
        arrived(g_buf.at[other, src], gd_r.at[src])

    halves = [g_buf[h].astype(F32) for h in range(2)]
    slot_out = [g[:, :pairs].reshape(slots, half).astype(BF16) for g in halves]
    slot_in_grad = [g[:, pairs:].reshape(slots, half).astype(BF16) for g in halves]

    def inner(values, against):
        return sum(
            dot(values[h], against[:, :, h * half : (h + 1) * half].reshape(image, half), 1, 1)
            for h in range(2)
        )

    comb_grad = inner(slot_out, og)
    disp_grad = inner(slot_in_grad, tok)
    combine, dispatch = comb[...], disp[...]
    comb_inner = jnp.sum(combine * comb_grad, axis=0, keepdims=True)
    disp_inner = jnp.sum(dispatch * disp_grad, axis=1, keepdims=True)
    logit_grad = combine * (comb_grad - comb_inner) + dispatch * (disp_grad - disp_inner)
    lg_b[...] = logit_grad.astype(BF16)

    in_order = dot(lg_b[...], slot_order, 0, 0).astype(BF16)
    block = width // (2 * plane)
    for x_to in range(nx):
        strip = pl.ds(pl.multiple_of(x_to * 2 * ny * block + core * ny * block, 16), ny * block)
        pg_send[x_to * ny : (x_to + 1) * ny] = dot(tokt[strip, :], in_order, 1, 0).reshape(ny, block, slots)
    for j in range(1, plane):
        to = shift(j)
        send(pg_send.at[to], pg_recv.at[xy], f1_s.at[j], f1_r.at[xy], device(to, z, core))

    own_rows = pl.ds(pl.multiple_of(core * rows, rows), rows)
    for h in range(2):
        cols = slice(h * half, (h + 1) * half)
        tg_ref[:, cols] = (
            dot(disp_b[:, own_rows], slot_in_grad[h], 0, 0) + dot(lg_b[:, own_rows], spt[:, cols], 0, 0)
        ).astype(BF16)

    total = pg_send[xy]
    for j in range(1, plane):
        src = shift(plane - j)
        arrived(pg_recv.at[src], f1_r.at[src])
        total = total + pg_recv[src]
    pad[...] = jnp.zeros_like(pad)
    pad[:block, :slots] = total
    per = slots // ring
    f2_send[...] = pad[...].T[:slots].reshape(ring, per, pad.shape[0])

    for j in range(1, ring):
        to = turn(at_ex + j)
        send(
            f2_send.at[to], f2_recv.at[z], f2_s.at[j], f2_r.at[z],
            device(xy, core * zl_n + lax.div(to, 2), lax.rem(to, 2)),
        )
    stays = zh == core

    def away(start):
        copy = pltpu.make_async_remote_copy(
            src_ref=f2_send.at[at_ex], dst_ref=f2_recv.at[z], send_sem=f2_s.at[0], recv_sem=f2_r.at[z],
            device_id=device(xy, core * zl_n + zl, core), device_id_type=MESH,
        )
        if start:
            copy.start()
        else:
            copy.wait_send()

    @pl.when(stays)
    def _():
        f2_recv[z] = f2_send[at_ex]

    @pl.when(jnp.logical_not(stays))
    def _():
        away(True)
        arrived(f2_recv.at[z], f2_r.at[z])

    for j in range(1, ring):
        src = turn(z + j)
        arrived(f2_recv.at[src], f2_r.at[src])
    summed = jnp.sum(f2_recv[...], axis=0)
    pad[:per] = summed
    pg_ref[...] = pad[...].T[:block, :per].astype(BF16)

    @pl.when(jnp.logical_not(stays))
    def _():
        away(False)

    for copy in started:
        copy.wait_send()


def shards(ny, tokens, out_grad, slot_param, w_in, w_out):
    dp, ex = lax.axis_size("dp"), lax.axis_size("expert")
    nx, zl_n = dp // (2 * ny), ex // 2
    plane, ring, pairs = nx * ny, 2 * zl_n, zl_n
    rows, width = tokens.shape
    slots = slot_param.shape[1]
    hidden = w_in.shape[1]
    half, image, images = width // 2, 2 * rows, ring * plane
    block, per = width // dp, slots // ex
    side = max(128, slots)
    dma = pltpu.SemaphoreType.DMA
    vmem = pltpu.VMEM
    return pl.pallas_call(
        functools.partial(kernel, nx, ny, zl_n),
        out_shape=(
            jax.ShapeDtypeStruct((rows, width), BF16),
            jax.ShapeDtypeStruct((block, per), BF16),
        ),
        in_specs=[pl.BlockSpec(memory_space=pl.ANY)] * 5,
        out_specs=(pl.BlockSpec(memory_space=pltpu.VMEM),) * 2,
        scratch_shapes=[
            vmem((2, rows, width), BF16),
            vmem((2, rows, width), BF16),
            vmem((width, slots), BF16),
            vmem((hidden, width), BF16),
            vmem((hidden, width), BF16),
            vmem((slots, width), BF16),
            vmem((width, image), BF16),
            vmem((slots, image), F32),
            vmem((slots, image), F32),
            vmem((slots, image), BF16),
            vmem((slots, image), BF16),
            vmem((plane, 2 * pairs, half), BF16),
            vmem((plane, 2 * pairs, half), BF16),
            vmem((pairs, 2, plane, half), BF16),
            vmem((2, 2, ring, plane, half), BF16),
            vmem((images, hidden), BF16),
            vmem((images, hidden), BF16),
            vmem((2, ring, plane, half), F32),
            vmem((2, ring, plane, half), BF16),
            vmem((2, ring, plane, half), BF16),
            vmem((2, ring, plane, half), BF16),
            vmem((2, ring, plane, half), BF16),
            vmem((pairs - 1, 2, plane, half), BF16),
            vmem((pairs, 2, plane, half), BF16),
            vmem((plane, 2 * pairs, half), BF16),
            vmem((2, plane, 2 * pairs, half), BF16),
            vmem((plane, block, slots), F32),
            vmem((plane, block, slots), F32),
            vmem((side, side), F32),
            vmem((ring, per, side), F32),
            vmem((ring, per, side), F32),
            dma((5,)),
            dma((2,)), dma((2,)),
            dma((plane,)), dma((plane,)),
            dma((pairs,)), dma((ring,)), dma((pairs,)),
            dma((ring,)), dma((ring,)),
            dma((2,)), dma((2,)),
            dma((pairs,)), dma((ring,)),
            dma((pairs,)), dma((pairs,)),
            dma((plane,)), dma((plane,)),
            dma((plane,)), dma((plane,)),
            dma((plane,)), dma((plane,)),
            dma((ring,)), dma((ring,)),
        ],
        compiler_params=pltpu.CompilerParams(
            collective_id=0, has_side_effects=True, vmem_limit_bytes=44 << 20
        ),
    )(tokens, out_grad, slot_param, w_in, w_out)


def solution(mesh):
    placed = (
        P(("dp", "expert"), None),
        P(("dp", "expert"), None),
        P(),
        P(("dp", "expert"), None, None),
        P(("dp", "expert"), None, None),
    )
    return jax.shard_map(
        functools.partial(shards, PLANE_Y),
        mesh=mesh,
        in_specs=placed,
        out_specs=(P(("dp", "expert"), None), P("dp", "expert")),
        check_vma=False,
    )
```

```python
import functools

import jax
import jax.numpy as jnp
from jax import lax
from jax.experimental import pallas as pl
from jax.experimental.pallas import tpu as pltpu
from jax.sharding import PartitionSpec as P

MESH = pl.DeviceIdType.MESH
PLANE_Y = 4
GROUPS = ((4, 8), (0, 4))
LOOK = True

gelu_scale = 0.7978845608
gelu_cubic = 0.044715

F32 = jnp.float32
BF16 = jnp.bfloat16


def gelu_parts(pre_act):
    inner_arg = gelu_scale * (pre_act + gelu_cubic * pre_act * pre_act * pre_act)
    tangent = jnp.tanh(inner_arg)
    gelu_value = 0.5 * pre_act * (1.0 + tangent)
    gelu_slope = 0.5 * (1.0 + tangent) + 0.5 * pre_act * (1.0 - tangent * tangent) * gelu_scale * (
        1.0 + 3.0 * gelu_cubic * pre_act * pre_act
    )
    return (gelu_value, gelu_slope)


def dot(a, b, ca, cb):
    return lax.dot_general(a, b, (((ca,), (cb,)), ((), ())), preferred_element_type=F32)


def tiles(extent, step=256):
    return [(at, min(step, extent - at)) for at in range(0, extent, step)]


def up16(n):
    return -(-n // 16) * 16


def log2(n):
    return n.bit_length() - 1


def kernel(
    nx, ny, zl_n,
    tok_hbm, og_hbm, sp_hbm, w1_hbm, w2_hbm,
    tg_ref, pg_ref,
    tok, og, sp, w1, w2, spt, tokt, disp, comb, disp_b, lg_b,
    s_buf, r_buf, t_buf, x_buf, gv, pgd, p_buf, o_send, o_recv, u_buf, v_buf, q_buf, b_buf, c_buf, g_buf,
    back_buf, pg_send, pg_recv, pad, f2_send, f2_recv,
    load_sem, swap_s, swap_r, p1_s, p1_r, p2_s, p2_r, rl_s, dd_s, dd_r, o_s, o_r,
    v_s, v_r, b_s, b_r, g_s, g_r, gd_s, gd_r, f1_s, f1_r, f2_s, f2_r,
):
    plane, ring, pairs = nx * ny, 2 * zl_n, zl_n
    reach = pairs - 1
    at_dp, at_ex = lax.axis_index("dp"), lax.axis_index("expert")
    core, zl = lax.rem(at_ex, 2), lax.div(at_ex, 2)
    y, xz = lax.rem(at_dp, ny), lax.div(at_dp, ny)
    zh, x = lax.rem(xz, 2), lax.div(xz, 2)
    z, xy = zh * zl_n + zl, x * ny + y
    sign = 2 * lax.rem(z, 2) - 1
    pair = lax.div(z, 2)
    other = 1 - core

    def turn(v):
        return lax.rem(v + 2 * ring, ring)

    def shift(j):
        return lax.rem(xy + j, plane)

    def device(xy_to, z_to, core_to):
        x_to, y_to = lax.div(xy_to, ny), lax.rem(xy_to, ny)
        return (
            (x_to * 2 + lax.div(z_to, zl_n)) * ny + y_to,
            lax.rem(z_to, zl_n) * 2 + core_to,
        )

    partner = device(xy, z, other)
    sibling = device(xy, turn(z - sign), core)
    started = []

    def send(src, dst, send_sem, recv_sem, to):
        copy = pltpu.make_async_remote_copy(
            src_ref=src, dst_ref=dst, send_sem=send_sem, recv_sem=recv_sem,
            device_id=to, device_id_type=MESH,
        )
        copy.start()
        started.append(copy)

    def arrived(dst, recv_sem):
        pltpu.make_async_remote_copy(
            src_ref=dst, dst_ref=dst, send_sem=recv_sem, recv_sem=recv_sem,
            device_id=partner, device_id_type=MESH,
        ).wait_recv()

    rows, width = tok_hbm.shape
    half = width // 2
    image = 2 * rows
    slots = plane * pairs
    own_cols = pl.ds(pl.multiple_of(core * half, half), half)

    barrier = pltpu.get_barrier_semaphore()
    pl.semaphore_signal(barrier, inc=1, device_id=partner, device_id_type=MESH)
    for j in range(1, plane):
        pl.semaphore_signal(barrier, inc=1, device_id=device(shift(j), z, core), device_id_type=MESH)
    for j in range(1, ring):
        for to in range(2):
            pl.semaphore_signal(
                barrier, inc=1, device_id=device(xy, turn(z + j), to), device_id_type=MESH
            )

    loads = [
        pltpu.make_async_copy(src, dst, load_sem.at[i])
        for i, (src, dst) in enumerate(
            [(tok_hbm, tok.at[core]), (og_hbm, og.at[core]), (sp_hbm, sp), (w1_hbm.at[0], w1), (w2_hbm.at[0], w2)]
        )
    ]
    for load in loads:
        load.start()

    place = lax.broadcasted_iota(jnp.int32, (slots, slots), 0)
    zl2_n = pairs // 2
    of_place = (
        (place >> log2(pairs * ny)) * (2 * ny * zl2_n)
        + ((place >> log2(zl2_n)) & 1) * (ny * zl2_n)
        + ((place >> log2(pairs)) & (ny - 1)) * zl2_n
        + (place & (zl2_n - 1))
    )
    across = lax.broadcasted_iota(jnp.int32, (slots, slots), 1)
    slot_order = (across == of_place).astype(F32).astype(BF16)
    cells = 2 * slots
    first_at = lax.broadcasted_iota(jnp.int32, (cells, cells), 0)
    second_at = lax.broadcasted_iota(jnp.int32, (cells, cells), 1)

    def by_source(at):
        kind = (at >> log2(plane)) & 1
        return (at & (plane - 1)) * (2 * pairs) + kind * pairs + (at >> log2(2 * plane))

    to_pairs = (second_at == by_source(first_at)).astype(F32).astype(BF16)
    to_sources = (first_at == by_source(second_at)).astype(F32).astype(BF16)
    pg_send[...] = jnp.zeros_like(pg_send)
    loads[2].wait()
    spt[...] = dot(slot_order, sp[...], 1, 1).astype(BF16)
    loads[0].wait()
    loads[1].wait()

    pl.semaphore_wait(barrier, plane + 2 * (ring - 1))
    send(tok.at[core], tok.at[core], swap_s.at[0], swap_r.at[0], partner)
    send(og.at[core], og.at[core], swap_s.at[1], swap_r.at[1], partner)
    arrived(tok.at[other], swap_r.at[0])

    tok_all = tok[...].reshape(image, width)
    logits = dot(spt[...], tok_all, 1, 1)
    col_exp = jnp.exp(logits - jnp.max(logits, axis=1, keepdims=True))
    dispatch = col_exp / jnp.sum(col_exp, axis=1, keepdims=True)
    disp[...] = dispatch
    disp_b[...] = dispatch.astype(BF16)
    slot_in = dot(disp_b[...], tok[:, :, own_cols].reshape(image, half), 1, 0)
    row_exp = jnp.exp(logits - jnp.max(logits, axis=0, keepdims=True))
    combine = row_exp / jnp.sum(row_exp, axis=0, keepdims=True)
    comb[...] = combine
    arrived(og.at[other], swap_r.at[1])
    slot_grad = dot(combine.astype(BF16), og[:, :, own_cols].reshape(image, half), 1, 0)
    s_buf[...] = jnp.concatenate(
        [slot_in.reshape(plane, pairs, half), slot_grad.reshape(plane, pairs, half)], axis=1
    ).astype(BF16)

    for j in range(1, plane):
        to = shift(j)
        send(s_buf.at[to], r_buf.at[xy], p1_s.at[j], p1_r.at[xy], device(to, z, core))
    r_buf[xy] = s_buf[xy]
    for j in range(1, plane):
        arrived(r_buf.at[shift(j)], p1_r.at[shift(j)])
    t_buf[...] = dot(to_pairs, r_buf[...].reshape(cells, half), 1, 0).astype(BF16).reshape(
        pairs, 2, plane, half
    )

    hops = [(sign, d) for d in range(1, pairs, 2)] + [(-sign, d) for d in range(2, pairs, 2)]
    hops.sort(key=lambda hop: -hop[1])
    for way, d in hops:
        to = turn(z + way * d)
        send(
            t_buf.at[lax.div(to, 2)], x_buf.at[core, :, 2 * d], p2_s.at[d], p2_r.at[2 * d],
            device(xy, to, core),
        )
    mine = t_buf.at[pair]
    send(mine, x_buf.at[core, :, 1], p2_s.at[0], p2_r.at[1], sibling)
    send(mine, x_buf.at[core, :, 0], dd_s.at[0], dd_r.at[0], partner)
    x_buf[core, :, 0] = t_buf[pair]
    images = ring * plane
    hidden = w1.shape[0]

    def take(at):
        slot = x_buf.at[core, :, at]
        arrived(slot, p2_r.at[at])
        if at > 1 and at % 2 == 0:
            send(slot, x_buf.at[core, :, at + 1], rl_s.at[at // 2], p2_r.at[at + 1], sibling)
        send(slot, slot, dd_s.at[at], dd_r.at[at], partner)

    def take_first(low, high):
        for j in range(high - 1, max(low, 1) - 1, -1):
            take(2 * j)

    def take_relayed(low, high):
        for j in range(high - 1, low - 1, -1):
            take(2 * j + 1)
        for at in range(2 * low, 2 * high):
            arrived(x_buf.at[other, :, at], dd_r.at[at])

    def expert(low, high):
        count = (high - low) * 2 * plane
        span = slice(2 * low, 2 * high)

        def both(kind, weights, at, n):
            return sum(
                dot(x_buf[h, kind, span].reshape(count, half), weights[at : at + n, h * half : (h + 1) * half], 1, 1)
                for h in range(2)
            )

        for at, n in tiles(hidden):
            gelu_value, gelu_slope = gelu_parts(both(0, w1, at, n))
            gv[:count, at : at + n] = gelu_value.astype(BF16)
            pgd[:count, at : at + n] = (both(1, w2, at, n) * gelu_slope).astype(BF16)

        def product(kind, whose, at, n):
            left, right = ((gv, w2), (pgd, w1))[kind]
            cols = pl.ds(pl.multiple_of(whose * half + at, 128), n)
            return dot(left[:count], right[:, cols], 1, 0).reshape(2 * (high - low), plane, n)

        for kind in range(2):
            for at, n in tiles(half):
                o_send[kind, span, :, at : at + n] = product(kind, other, at, n).astype(BF16)
        send(o_send.at[:, span], o_recv.at[:, span], o_s.at[low], o_r.at[low], partner)
        for kind in range(2):
            for at, n in tiles(half):
                p_buf[kind, span, :, at : at + n] = product(kind, core, at, n)

    def give(low, high):
        span = slice(2 * low, 2 * high)
        arrived(o_recv.at[:, span], o_r.at[low])
        for j in range(high - 1, low - 1, -1):
            at = 2 * j + 1
            u_buf[j] = (p_buf[:, at] + o_recv[:, at].astype(F32)).astype(BF16)
            send(u_buf.at[j], v_buf.at[j], v_s.at[j], v_r.at[j], sibling)

    def pass_back(low, high):
        for j in range(high - 1, low - 1, -1):
            arrived(v_buf.at[j], v_r.at[j])
            at = 2 * j
            whole = (p_buf[:, at] + o_recv[:, at].astype(F32) + v_buf[j].astype(F32)).astype(BF16)
            if j == 0:
                b_buf[pair] = whole
            else:
                q_buf[j] = whole
                send(q_buf.at[j], b_buf.at[pair], b_s.at[j], b_r.at[pair], device(xy, turn(z + sign * j), core))

    groups = [(low, min(high, pairs)) for low, high in GROUPS if low < pairs]
    take_first(*groups[0])
    for i, group in enumerate(groups):
        if LOOK and i + 1 < len(groups):
            take_first(*groups[i + 1])
        take_relayed(*group)
        if i == 0:
            loads[3].wait()
            loads[4].wait()
        expert(*group)
        if not LOOK and i + 1 < len(groups):
            take_first(*groups[i + 1])
        if i > 0:
            pass_back(*groups[i - 1])
        give(*group)
    pass_back(*groups[-1])

    for at, n in tiles(width, 128):
        tokt[at : at + n] = tok[:, :, at : at + n].reshape(image, n).astype(F32).T.astype(BF16)

    for j in range(1, pairs):
        src = lax.rem(pair + j, pairs)
        arrived(b_buf.at[src], b_r.at[src])
    c_buf[...] = dot(to_sources, b_buf[...].reshape(cells, half), 1, 0).astype(BF16).reshape(
        plane, 2 * pairs, half
    )

    for j in range(1, plane):
        to = shift(j)
        send(c_buf.at[to], g_buf.at[xy], g_s.at[j], g_r.at[xy], device(to, z, core))
    g_buf[xy] = c_buf[xy]
    for j in range(1, plane):
        src = shift(plane - j)
        arrived(g_buf.at[src], g_r.at[src])
    came = g_buf[...].astype(F32)
    for kind in (1, 0):
        back_buf[kind, core] = came[:, kind * pairs : (kind + 1) * pairs].reshape(slots, half).astype(BF16)
        mine = back_buf.at[kind, core]
        send(mine, mine, gd_s.at[kind], gd_r.at[kind], partner)

    def inner(kind, against):
        arrived(back_buf.at[kind, other], gd_r.at[kind])
        return sum(
            dot(back_buf[kind, h], against[:, :, h * half : (h + 1) * half].reshape(image, half), 1, 1)
            for h in range(2)
        )

    disp_grad = inner(1, tok)
    comb_grad = inner(0, og)
    combine = comb[...]
    dispatch = disp[...]
    comb_inner = jnp.sum(combine * comb_grad, axis=0, keepdims=True)
    logit_grad = combine * (comb_grad - comb_inner) + dispatch * (disp_grad - jnp.sum(dispatch * disp_grad, axis=1, keepdims=True))
    lg_b[...] = logit_grad.astype(BF16)

    in_order = dot(lg_b[...], slot_order, 0, 0).astype(BF16)
    block = width // (2 * plane)
    for x_to in range(nx):
        strip_at = pl.ds(pl.multiple_of(x_to * 2 * ny * block + core * ny * block, 16), ny * block)
        pg_send[x_to * ny : (x_to + 1) * ny, :block] = (
            dot(tokt[strip_at, :], in_order, 1, 0).reshape(ny, block, slots).astype(BF16)
        )
    for j in range(1, plane):
        to = shift(j)
        send(pg_send.at[to], pg_recv.at[xy], f1_s.at[j], f1_r.at[xy], device(to, z, core))

    own_rows = pl.ds(pl.multiple_of(core * rows, rows), rows)
    for h in range(2):
        cols = slice(h * half, (h + 1) * half)
        tg_ref[:, cols] = (
            dot(disp_b[:, own_rows], back_buf[1, h], 0, 0) + dot(lg_b[:, own_rows], spt[:, cols], 0, 0)
        ).astype(BF16)

    total = pg_send[xy].astype(F32)
    for j in range(1, plane):
        src = shift(plane - j)
        arrived(pg_recv.at[src], f1_r.at[src])
        total = total + pg_recv[src].astype(F32)
    pad[...] = jnp.zeros_like(pad)
    pad[:block, :slots] = total[:block]
    per = slots // ring
    f2_send[...] = pad[...].T[:slots].reshape(ring, per, pad.shape[0])

    for j in sorted(range(1, ring), key=lambda j: -min(j, ring - j)):
        to = turn(at_ex + j)
        send(
            f2_send.at[to], f2_recv.at[z], f2_s.at[j], f2_r.at[z],
            device(xy, core * zl_n + lax.div(to, 2), lax.rem(to, 2)),
        )
    stays = zh == core

    def away(start):
        copy = pltpu.make_async_remote_copy(
            src_ref=f2_send.at[at_ex], dst_ref=f2_recv.at[z], send_sem=f2_s.at[0], recv_sem=f2_r.at[z],
            device_id=device(xy, core * zl_n + zl, core), device_id_type=MESH,
        )
        if start:
            copy.start()
        else:
            copy.wait_send()

    @pl.when(stays)
    def _():
        f2_recv[z] = f2_send[at_ex]

    @pl.when(jnp.logical_not(stays))
    def _():
        away(True)
        arrived(f2_recv.at[z], f2_r.at[z])

    for j in range(1, ring):
        src = turn(z + j)
        arrived(f2_recv.at[src], f2_r.at[src])
    pg_ref[...] = jnp.sum(f2_recv[...], axis=0)[:, :block].astype(BF16)

    @pl.when(jnp.logical_not(stays))
    def _():
        away(False)

    for copy in started:
        copy.wait_send()


def shards(ny, tokens, out_grad, slot_param, w_in, w_out):
    dp, ex = lax.axis_size("dp"), lax.axis_size("expert")
    nx, zl_n = dp // (2 * ny), ex // 2
    plane, ring, pairs = nx * ny, 2 * zl_n, zl_n
    rows, width = tokens.shape
    slots = slot_param.shape[1]
    hidden = w_in.shape[1]
    half, image, images = width // 2, 2 * rows, ring * plane
    block, per = width // dp, slots // ex
    side = max(128, slots)
    dma = pltpu.SemaphoreType.DMA
    vmem = pltpu.VMEM
    token_grad, param_grad = pl.pallas_call(
        functools.partial(kernel, nx, ny, zl_n),
        out_shape=(
            jax.ShapeDtypeStruct((rows, width), BF16),
            jax.ShapeDtypeStruct((per, block), BF16),
        ),
        in_specs=[pl.BlockSpec(memory_space=pl.ANY)] * 5,
        out_specs=(pl.BlockSpec(memory_space=pltpu.VMEM),) * 2,
        scratch_shapes=[
            vmem((2, rows, width), BF16),
            vmem((2, rows, width), BF16),
            vmem((width, slots), BF16),
            vmem((hidden, width), BF16),
            vmem((hidden, width), BF16),
            vmem((slots, width), BF16),
            vmem((width, image), BF16),
            vmem((slots, image), F32),
            vmem((slots, image), F32),
            vmem((slots, image), BF16),
            vmem((slots, image), BF16),
            vmem((plane, 2 * pairs, half), BF16),
            vmem((plane, 2 * pairs, half), BF16),
            vmem((pairs, 2, plane, half), BF16),
            vmem((2, 2, ring, plane, half), BF16),
            vmem((images, hidden), BF16),
            vmem((images, hidden), BF16),
            vmem((2, ring, plane, half), F32),
            vmem((2, ring, plane, half), BF16),
            vmem((2, ring, plane, half), BF16),
            vmem((pairs, 2, plane, half), BF16),
            vmem((pairs, 2, plane, half), BF16),
            vmem((pairs, 2, plane, half), BF16),
            vmem((pairs, 2, plane, half), BF16),
            vmem((plane, 2 * pairs, half), BF16),
            vmem((plane, 2 * pairs, half), BF16),
            vmem((2, 2, slots, half), BF16),
            vmem((plane, up16(block), slots), BF16),
            vmem((plane, up16(block), slots), BF16),
            vmem((side, side), F32),
            vmem((ring, per, side), F32),
            vmem((ring, per, side), F32),
            dma((5,)),
            dma((2,)), dma((2,)),
            dma((plane,)), dma((plane,)),
            dma((pairs,)), dma((ring,)), dma((pairs,)),
            dma((ring,)), dma((ring,)),
            dma((pairs,)), dma((pairs,)),
            dma((pairs,)), dma((pairs,)),
            dma((pairs,)), dma((pairs,)),
            dma((plane,)), dma((plane,)),
            dma((2,)), dma((2,)),
            dma((plane,)), dma((plane,)),
            dma((ring,)), dma((ring,)),
        ],
        compiler_params=pltpu.CompilerParams(
            collective_id=0, has_side_effects=True, vmem_limit_bytes=60 << 20
        ),
    )(tokens, out_grad, slot_param, w_in, w_out)
    return token_grad, param_grad.T


def solution(mesh):
    placed = (
        P(("dp", "expert"), None),
        P(("dp", "expert"), None),
        P(),
        P(("dp", "expert"), None, None),
        P(("dp", "expert"), None, None),
    )
    return jax.shard_map(
        functools.partial(shards, PLANE_Y),
        mesh=mesh,
        in_specs=placed,
        out_specs=(P(("dp", "expert"), None), P("dp", "expert")),
        check_vma=False,
    )
```

```python
import functools

import jax
import jax.numpy as jnp
from jax import lax
from jax.experimental import pallas as pl
from jax.experimental.pallas import tpu as pltpu
from jax.sharding import PartitionSpec as P

MESH = pl.DeviceIdType.MESH
PLANE_Y = 4
GROUPS = ((4, 8), (0, 4))
LOOK = True

gelu_scale = 0.7978845608
gelu_cubic = 0.044715

F32 = jnp.float32
BF16 = jnp.bfloat16


def gelu_parts(pre_act):
    inner_arg = gelu_scale * (pre_act + gelu_cubic * pre_act * pre_act * pre_act)
    tangent = jnp.tanh(inner_arg)
    gelu_value = 0.5 * pre_act * (1.0 + tangent)
    gelu_slope = 0.5 * (1.0 + tangent) + 0.5 * pre_act * (1.0 - tangent * tangent) * gelu_scale * (
        1.0 + 3.0 * gelu_cubic * pre_act * pre_act
    )
    return (gelu_value, gelu_slope)


def dot(a, b, ca, cb):
    return lax.dot_general(a, b, (((ca,), (cb,)), ((), ())), preferred_element_type=F32)


def tiles(extent, step=256):
    return [(at, min(step, extent - at)) for at in range(0, extent, step)]


def up16(n):
    return -(-n // 16) * 16


def log2(n):
    return n.bit_length() - 1


def kernel(
    nx, ny, zl_n,
    tok_hbm, og_hbm, sp_hbm, w1_hbm, w2_hbm,
    tg_ref, pg_ref,
    tok, og, sp, w1, w2, spt, tokt, disp, comb, disp_b, lg_b,
    s_buf, r_buf, t_buf, x_buf, gv, pgd, p_buf, o_send, o_recv, u_buf, v_buf, q_buf, b_buf, c_buf, g_buf,
    back_buf, pg_send, pg_recv, pad, f2_send, f2_recv,
    load_sem, swap_s, swap_r, p1_s, p1_r, p2_s, p2_r, rl_s, dd_s, dd_r, o_s, o_r,
    v_s, v_r, b_s, b_r, g_s, g_r, gd_s, gd_r, f1_s, f1_r, f2_s, f2_r, known,
):
    plane, ring, pairs = nx * ny, 2 * zl_n, zl_n
    reach = pairs - 1
    at_dp, at_ex = lax.axis_index("dp"), lax.axis_index("expert")
    core, zl = lax.rem(at_ex, 2), lax.div(at_ex, 2)
    y, xz = lax.rem(at_dp, ny), lax.div(at_dp, ny)
    zh, x = lax.rem(xz, 2), lax.div(xz, 2)
    z, xy = zh * zl_n + zl, x * ny + y
    sign = 2 * lax.rem(z, 2) - 1
    pair = lax.div(z, 2)
    other = 1 - core

    def turn(v):
        return lax.rem(v + 2 * ring, ring)

    def shift(j):
        return lax.rem(xy + j, plane)

    def device(xy_to, z_to, core_to):
        x_to, y_to = lax.div(xy_to, ny), lax.rem(xy_to, ny)
        return (
            (x_to * 2 + lax.div(z_to, zl_n)) * ny + y_to,
            lax.rem(z_to, zl_n) * 2 + core_to,
        )

    partner = device(xy, z, other)
    sibling = device(xy, turn(z - sign), core)
    started = []

    def send(src, dst, send_sem, recv_sem, to):
        copy = pltpu.make_async_remote_copy(
            src_ref=src, dst_ref=dst, send_sem=send_sem, recv_sem=recv_sem,
            device_id=to, device_id_type=MESH,
        )
        copy.start()
        started.append(copy)

    def arrived(dst, recv_sem):
        pltpu.make_async_remote_copy(
            src_ref=dst, dst_ref=dst, send_sem=recv_sem, recv_sem=recv_sem,
            device_id=partner, device_id_type=MESH,
        ).wait_recv()

    rows, width = tok_hbm.shape
    half = width // 2
    image = 2 * rows
    slots = plane * pairs
    own_cols = pl.ds(pl.multiple_of(core * half, half), half)

    barrier = pltpu.get_barrier_semaphore()
    pl.semaphore_signal(barrier, inc=1, device_id=partner, device_id_type=MESH)
    for j in range(1, plane):
        pl.semaphore_signal(barrier, inc=1, device_id=device(shift(j), z, core), device_id_type=MESH)
    for step in (1, ring - 1):
        pl.semaphore_signal(barrier, inc=1, device_id=device(xy, turn(z + step), core), device_id_type=MESH)

    def tell(i):
        for step in (1 << i, ring - (1 << i)):
            pl.semaphore_signal(
                known.at[i], inc=1, device_id=device(xy, turn(z + step), core), device_id_type=MESH
            )

    rounds = log2(ring) - 1
    loads = [
        pltpu.make_async_copy(src, dst, load_sem.at[i])
        for i, (src, dst) in enumerate(
            [(tok_hbm, tok.at[core]), (og_hbm, og.at[core]), (sp_hbm, sp), (w1_hbm.at[0], w1), (w2_hbm.at[0], w2)]
        )
    ]
    for load in loads:
        load.start()

    place = lax.broadcasted_iota(jnp.int32, (slots, slots), 0)
    zl2_n = pairs // 2
    of_place = (
        (place >> log2(pairs * ny)) * (2 * ny * zl2_n)
        + ((place >> log2(zl2_n)) & 1) * (ny * zl2_n)
        + ((place >> log2(pairs)) & (ny - 1)) * zl2_n
        + (place & (zl2_n - 1))
    )
    across = lax.broadcasted_iota(jnp.int32, (slots, slots), 1)
    slot_order = (across == of_place).astype(F32).astype(BF16)
    cells = 2 * slots
    first_at = lax.broadcasted_iota(jnp.int32, (cells, cells), 0)
    second_at = lax.broadcasted_iota(jnp.int32, (cells, cells), 1)

    def by_source(at):
        kind = (at >> log2(plane)) & 1
        return (at & (plane - 1)) * (2 * pairs) + kind * pairs + (at >> log2(2 * plane))

    to_pairs = (second_at == by_source(first_at)).astype(F32).astype(BF16)
    to_sources = (first_at == by_source(second_at)).astype(F32).astype(BF16)
    pg_send[...] = jnp.zeros_like(pg_send)
    loads[2].wait()
    spt[...] = dot(slot_order, sp[...], 1, 1).astype(BF16)
    loads[0].wait()
    loads[1].wait()

    pl.semaphore_wait(barrier, plane + 2)
    tell(0)
    send(tok.at[core], tok.at[core], swap_s.at[0], swap_r.at[0], partner)
    send(og.at[core], og.at[core], swap_s.at[1], swap_r.at[1], partner)
    arrived(tok.at[other], swap_r.at[0])

    tok_all = tok[...].reshape(image, width)
    logits = dot(spt[...], tok_all, 1, 1)
    col_exp = jnp.exp(logits - jnp.max(logits, axis=1, keepdims=True))
    dispatch = col_exp / jnp.sum(col_exp, axis=1, keepdims=True)
    disp[...] = dispatch
    disp_b[...] = dispatch.astype(BF16)
    slot_in = dot(disp_b[...], tok[:, :, own_cols].reshape(image, half), 1, 0)
    row_exp = jnp.exp(logits - jnp.max(logits, axis=0, keepdims=True))
    combine = row_exp / jnp.sum(row_exp, axis=0, keepdims=True)
    comb[...] = combine
    arrived(og.at[other], swap_r.at[1])
    slot_grad = dot(combine.astype(BF16), og[:, :, own_cols].reshape(image, half), 1, 0)
    s_buf[...] = jnp.concatenate(
        [slot_in.reshape(plane, pairs, half), slot_grad.reshape(plane, pairs, half)], axis=1
    ).astype(BF16)

    for j in range(1, plane):
        to = shift(j)
        send(s_buf.at[to], r_buf.at[xy], p1_s.at[j], p1_r.at[xy], device(to, z, core))
    r_buf[xy] = s_buf[xy]
    for i in range(1, rounds):
        pl.semaphore_wait(known.at[i - 1], 2)
        tell(i)
    for j in range(1, plane):
        arrived(r_buf.at[shift(j)], p1_r.at[shift(j)])
    t_buf[...] = dot(to_pairs, r_buf[...].reshape(cells, half), 1, 0).astype(BF16).reshape(
        pairs, 2, plane, half
    )
    pl.semaphore_wait(known.at[rounds - 1], 2)

    hops = [(sign, d) for d in range(1, pairs, 2)] + [(-sign, d) for d in range(2, pairs, 2)]
    hops.sort(key=lambda hop: -hop[1])
    for way, d in hops:
        to = turn(z + way * d)
        send(
            t_buf.at[lax.div(to, 2)], x_buf.at[core, :, 2 * d], p2_s.at[d], p2_r.at[2 * d],
            device(xy, to, core),
        )
    mine = t_buf.at[pair]
    send(mine, x_buf.at[core, :, 1], p2_s.at[0], p2_r.at[1], sibling)
    send(mine, x_buf.at[core, :, 0], dd_s.at[0], dd_r.at[0], partner)
    x_buf[core, :, 0] = t_buf[pair]
    images = ring * plane
    hidden = w1.shape[0]

    def take(at):
        slot = x_buf.at[core, :, at]
        arrived(slot, p2_r.at[at])
        if at > 1 and at % 2 == 0:
            send(slot, x_buf.at[core, :, at + 1], rl_s.at[at // 2], p2_r.at[at + 1], sibling)
        send(slot, slot, dd_s.at[at], dd_r.at[at], partner)

    def take_first(low, high):
        for j in range(high - 1, max(low, 1) - 1, -1):
            take(2 * j)

    def take_relayed(low, high):
        for j in range(high - 1, low - 1, -1):
            take(2 * j + 1)
        for at in range(2 * low, 2 * high):
            arrived(x_buf.at[other, :, at], dd_r.at[at])

    def expert(low, high):
        count = (high - low) * 2 * plane
        span = slice(2 * low, 2 * high)

        def both(kind, weights, at, n):
            return sum(
                dot(x_buf[h, kind, span].reshape(count, half), weights[at : at + n, h * half : (h + 1) * half], 1, 1)
                for h in range(2)
            )

        for at, n in tiles(hidden):
            gelu_value, gelu_slope = gelu_parts(both(0, w1, at, n))
            gv[:count, at : at + n] = gelu_value.astype(BF16)
            pgd[:count, at : at + n] = (both(1, w2, at, n) * gelu_slope).astype(BF16)

        def product(kind, whose, at, n):
            left, right = ((gv, w2), (pgd, w1))[kind]
            cols = pl.ds(pl.multiple_of(whose * half + at, 128), n)
            return dot(left[:count], right[:, cols], 1, 0).reshape(2 * (high - low), plane, n)

        for kind in range(2):
            for at, n in tiles(half):
                o_send[kind, span, :, at : at + n] = product(kind, other, at, n).astype(BF16)
        send(o_send.at[:, span], o_recv.at[:, span], o_s.at[low], o_r.at[low], partner)
        for kind in range(2):
            for at, n in tiles(half):
                p_buf[kind, span, :, at : at + n] = product(kind, core, at, n)

    def give(low, high):
        span = slice(2 * low, 2 * high)
        arrived(o_recv.at[:, span], o_r.at[low])
        for j in range(high - 1, low - 1, -1):
            at = 2 * j + 1
            u_buf[j] = (p_buf[:, at] + o_recv[:, at].astype(F32)).astype(BF16)
            send(u_buf.at[j], v_buf.at[j], v_s.at[j], v_r.at[j], sibling)

    def pass_back(low, high):
        for j in range(high - 1, low - 1, -1):
            arrived(v_buf.at[j], v_r.at[j])
            at = 2 * j
            whole = (p_buf[:, at] + o_recv[:, at].astype(F32) + v_buf[j].astype(F32)).astype(BF16)
            if j == 0:
                b_buf[pair] = whole
            else:
                q_buf[j] = whole
                send(q_buf.at[j], b_buf.at[pair], b_s.at[j], b_r.at[pair], device(xy, turn(z + sign * j), core))

    groups = [(low, min(high, pairs)) for low, high in GROUPS if low < pairs]
    take_first(*groups[0])
    for i, group in enumerate(groups):
        if LOOK and i + 1 < len(groups):
            take_first(*groups[i + 1])
        take_relayed(*group)
        if i == 0:
            loads[3].wait()
            loads[4].wait()
        expert(*group)
        if not LOOK and i + 1 < len(groups):
            take_first(*groups[i + 1])
        if i > 0:
            pass_back(*groups[i - 1])
        give(*group)
    pass_back(*groups[-1])

    for at, n in tiles(width, 128):
        tokt[at : at + n] = tok[:, :, at : at + n].reshape(image, n).astype(F32).T.astype(BF16)

    for j in range(1, pairs):
        src = lax.rem(pair + j, pairs)
        arrived(b_buf.at[src], b_r.at[src])
    c_buf[...] = dot(to_sources, b_buf[...].reshape(cells, half), 1, 0).astype(BF16).reshape(
        plane, 2 * pairs, half
    )

    for j in range(1, plane):
        to = shift(j)
        send(c_buf.at[to], g_buf.at[xy], g_s.at[j], g_r.at[xy], device(to, z, core))
    g_buf[xy] = c_buf[xy]
    for j in range(1, plane):
        src = shift(plane - j)
        arrived(g_buf.at[src], g_r.at[src])
    came = g_buf[...].astype(F32)
    for kind in (1, 0):
        back_buf[kind, core] = came[:, kind * pairs : (kind + 1) * pairs].reshape(slots, half).astype(BF16)
        mine = back_buf.at[kind, core]
        send(mine, mine, gd_s.at[kind], gd_r.at[kind], partner)

    def inner(kind, against):
        arrived(back_buf.at[kind, other], gd_r.at[kind])
        return sum(
            dot(back_buf[kind, h], against[:, :, h * half : (h + 1) * half].reshape(image, half), 1, 1)
            for h in range(2)
        )

    disp_grad = inner(1, tok)
    comb_grad = inner(0, og)
    combine = comb[...]
    dispatch = disp[...]
    comb_inner = jnp.sum(combine * comb_grad, axis=0, keepdims=True)
    logit_grad = combine * (comb_grad - comb_inner) + dispatch * (disp_grad - jnp.sum(dispatch * disp_grad, axis=1, keepdims=True))
    lg_b[...] = logit_grad.astype(BF16)

    in_order = dot(lg_b[...], slot_order, 0, 0).astype(BF16)
    block = width // (2 * plane)
    for x_to in range(nx):
        strip_at = pl.ds(pl.multiple_of(x_to * 2 * ny * block + core * ny * block, 16), ny * block)
        pg_send[x_to * ny : (x_to + 1) * ny, :block] = (
            dot(tokt[strip_at, :], in_order, 1, 0).reshape(ny, block, slots).astype(BF16)
        )
    for j in range(1, plane):
        to = shift(j)
        send(pg_send.at[to], pg_recv.at[xy], f1_s.at[j], f1_r.at[xy], device(to, z, core))

    own_rows = pl.ds(pl.multiple_of(core * rows, rows), rows)
    for h in range(2):
        cols = slice(h * half, (h + 1) * half)
        tg_ref[:, cols] = (
            dot(disp_b[:, own_rows], back_buf[1, h], 0, 0) + dot(lg_b[:, own_rows], spt[:, cols], 0, 0)
        ).astype(BF16)

    total = pg_send[xy].astype(F32)
    for j in range(1, plane):
        src = shift(plane - j)
        arrived(pg_recv.at[src], f1_r.at[src])
        total = total + pg_recv[src].astype(F32)
    pad[...] = jnp.zeros_like(pad)
    pad[:block, :slots] = total[:block]
    per = slots // ring
    f2_send[...] = pad[...].T[:slots].reshape(ring, per, pad.shape[0])

    for j in sorted(range(1, ring), key=lambda j: -min(j, ring - j)):
        to = turn(at_ex + j)
        send(
            f2_send.at[to], f2_recv.at[z], f2_s.at[j], f2_r.at[z],
            device(xy, core * zl_n + lax.div(to, 2), lax.rem(to, 2)),
        )
    stays = zh == core

    def away(start):
        copy = pltpu.make_async_remote_copy(
            src_ref=f2_send.at[at_ex], dst_ref=f2_recv.at[z], send_sem=f2_s.at[0], recv_sem=f2_r.at[z],
            device_id=device(xy, core * zl_n + zl, core), device_id_type=MESH,
        )
        if start:
            copy.start()
        else:
            copy.wait_send()

    @pl.when(stays)
    def _():
        f2_recv[z] = f2_send[at_ex]

    @pl.when(jnp.logical_not(stays))
    def _():
        away(True)
        arrived(f2_recv.at[z], f2_r.at[z])

    for j in range(1, ring):
        src = turn(z + j)
        arrived(f2_recv.at[src], f2_r.at[src])
    pg_ref[...] = jnp.sum(f2_recv[...], axis=0)[:, :block].astype(BF16)

    @pl.when(jnp.logical_not(stays))
    def _():
        away(False)

    for copy in started:
        copy.wait_send()


def shards(ny, tokens, out_grad, slot_param, w_in, w_out):
    dp, ex = lax.axis_size("dp"), lax.axis_size("expert")
    nx, zl_n = dp // (2 * ny), ex // 2
    plane, ring, pairs = nx * ny, 2 * zl_n, zl_n
    rows, width = tokens.shape
    slots = slot_param.shape[1]
    hidden = w_in.shape[1]
    half, image, images = width // 2, 2 * rows, ring * plane
    block, per = width // dp, slots // ex
    side = max(128, slots)
    dma = pltpu.SemaphoreType.DMA
    vmem = pltpu.VMEM
    token_grad, param_grad = pl.pallas_call(
        functools.partial(kernel, nx, ny, zl_n),
        out_shape=(
            jax.ShapeDtypeStruct((rows, width), BF16),
            jax.ShapeDtypeStruct((per, block), BF16),
        ),
        in_specs=[pl.BlockSpec(memory_space=pl.ANY)] * 5,
        out_specs=(pl.BlockSpec(memory_space=pltpu.VMEM),) * 2,
        scratch_shapes=[
            vmem((2, rows, width), BF16),
            vmem((2, rows, width), BF16),
            vmem((width, slots), BF16),
            vmem((hidden, width), BF16),
            vmem((hidden, width), BF16),
            vmem((slots, width), BF16),
            vmem((width, image), BF16),
            vmem((slots, image), F32),
            vmem((slots, image), F32),
            vmem((slots, image), BF16),
            vmem((slots, image), BF16),
            vmem((plane, 2 * pairs, half), BF16),
            vmem((plane, 2 * pairs, half), BF16),
            vmem((pairs, 2, plane, half), BF16),
            vmem((2, 2, ring, plane, half), BF16),
            vmem((images, hidden), BF16),
            vmem((images, hidden), BF16),
            vmem((2, ring, plane, half), F32),
            vmem((2, ring, plane, half), BF16),
            vmem((2, ring, plane, half), BF16),
            vmem((pairs, 2, plane, half), BF16),
            vmem((pairs, 2, plane, half), BF16),
            vmem((pairs, 2, plane, half), BF16),
            vmem((pairs, 2, plane, half), BF16),
            vmem((plane, 2 * pairs, half), BF16),
            vmem((plane, 2 * pairs, half), BF16),
            vmem((2, 2, slots, half), BF16),
            vmem((plane, up16(block), slots), BF16),
            vmem((plane, up16(block), slots), BF16),
            vmem((side, side), F32),
            vmem((ring, per, side), F32),
            vmem((ring, per, side), F32),
            dma((5,)),
            dma((2,)), dma((2,)),
            dma((plane,)), dma((plane,)),
            dma((pairs,)), dma((ring,)), dma((pairs,)),
            dma((ring,)), dma((ring,)),
            dma((pairs,)), dma((pairs,)),
            dma((pairs,)), dma((pairs,)),
            dma((pairs,)), dma((pairs,)),
            dma((plane,)), dma((plane,)),
            dma((2,)), dma((2,)),
            dma((plane,)), dma((plane,)),
            dma((ring,)), dma((ring,)),
            pltpu.SemaphoreType.REGULAR((max(1, ring.bit_length() - 2),)),
        ],
        compiler_params=pltpu.CompilerParams(
            collective_id=0, has_side_effects=True, vmem_limit_bytes=60 << 20
        ),
    )(tokens, out_grad, slot_param, w_in, w_out)
    return token_grad, param_grad.T


def solution(mesh):
    placed = (
        P(("dp", "expert"), None),
        P(("dp", "expert"), None),
        P(),
        P(("dp", "expert"), None, None),
        P(("dp", "expert"), None, None),
    )
    return jax.shard_map(
        functools.partial(shards, PLANE_Y),
        mesh=mesh,
        in_specs=placed,
        out_specs=(P(("dp", "expert"), None), P("dp", "expert")),
        check_vma=False,
    )
```

```python
import functools

import jax
import jax.numpy as jnp
from jax import lax
from jax.experimental import pallas as pl
from jax.experimental.pallas import tpu as pltpu
from jax.sharding import PartitionSpec as P

MESH = pl.DeviceIdType.MESH
PLANE_Y = 4
GROUPS = ((3, 8), (0, 3))
LOOK = True

gelu_scale = 0.7978845608
gelu_cubic = 0.044715

F32 = jnp.float32
BF16 = jnp.bfloat16


def gelu_parts(pre_act):
    inner_arg = gelu_scale * (pre_act + gelu_cubic * pre_act * pre_act * pre_act)
    tangent = jnp.tanh(inner_arg)
    gelu_value = 0.5 * pre_act * (1.0 + tangent)
    gelu_slope = 0.5 * (1.0 + tangent) + 0.5 * pre_act * (1.0 - tangent * tangent) * gelu_scale * (
        1.0 + 3.0 * gelu_cubic * pre_act * pre_act
    )
    return (gelu_value, gelu_slope)


def dot(a, b, ca, cb):
    return lax.dot_general(a, b, (((ca,), (cb,)), ((), ())), preferred_element_type=F32)


def tiles(extent, step=256):
    return [(at, min(step, extent - at)) for at in range(0, extent, step)]


def up16(n):
    return -(-n // 16) * 16


def log2(n):
    return n.bit_length() - 1


def kernel(
    nx, ny, zl_n,
    tok_hbm, og_hbm, sp_hbm, w1_hbm, w2_hbm,
    tg_ref, pg_ref,
    tok, og, sp, w1, w2, spt, tokt, disp, comb, disp_b, lg_b,
    s_buf, r_buf, t_buf, x_buf, gv, pgd, p_buf, o_send, o_recv, u_buf, v_buf, q_buf, b_buf, c_buf, g_buf,
    back_buf, pg_send, pg_recv, pad, f2_send, f2_recv,
    load_sem, swap_s, swap_r, p1_s, p1_r, p2_s, p2_r, rl_s, dd_s, dd_r, o_s, o_r,
    v_s, v_r, b_s, b_r, g_s, g_r, gd_s, gd_r, f1_s, f1_r, f2_s, f2_r, known, tg,
):
    plane, ring, pairs = nx * ny, 2 * zl_n, zl_n
    reach = pairs - 1
    at_dp, at_ex = lax.axis_index("dp"), lax.axis_index("expert")
    core, zl = lax.rem(at_ex, 2), lax.div(at_ex, 2)
    y, xz = lax.rem(at_dp, ny), lax.div(at_dp, ny)
    zh, x = lax.rem(xz, 2), lax.div(xz, 2)
    z, xy = zh * zl_n + zl, x * ny + y
    sign = 2 * lax.rem(z, 2) - 1
    pair = lax.div(z, 2)
    other = 1 - core

    def turn(v):
        return lax.rem(v + 2 * ring, ring)

    def shift(j):
        return lax.rem(xy + j, plane)

    def device(xy_to, z_to, core_to):
        x_to, y_to = lax.div(xy_to, ny), lax.rem(xy_to, ny)
        return (
            (x_to * 2 + lax.div(z_to, zl_n)) * ny + y_to,
            lax.rem(z_to, zl_n) * 2 + core_to,
        )

    partner = device(xy, z, other)
    sibling = device(xy, turn(z - sign), core)
    started = []

    def send(src, dst, send_sem, recv_sem, to):
        copy = pltpu.make_async_remote_copy(
            src_ref=src, dst_ref=dst, send_sem=send_sem, recv_sem=recv_sem,
            device_id=to, device_id_type=MESH,
        )
        copy.start()
        started.append(copy)

    def arrived(dst, recv_sem):
        pltpu.make_async_remote_copy(
            src_ref=dst, dst_ref=dst, send_sem=recv_sem, recv_sem=recv_sem,
            device_id=partner, device_id_type=MESH,
        ).wait_recv()

    rows, width = tok_hbm.shape
    half = width // 2
    image = 2 * rows
    slots = plane * pairs
    own_cols = pl.ds(pl.multiple_of(core * half, half), half)

    barrier = pltpu.get_barrier_semaphore()
    pl.semaphore_signal(barrier, inc=1, device_id=partner, device_id_type=MESH)
    for j in range(1, plane):
        pl.semaphore_signal(barrier, inc=1, device_id=device(shift(j), z, core), device_id_type=MESH)
    near = 2 if ring >= 8 else 1
    for step in [way for k in range(near) for way in (1 << k, ring - (1 << k))]:
        pl.semaphore_signal(barrier, inc=1, device_id=device(xy, turn(z + step), core), device_id_type=MESH)

    def tell(i):
        for step in (1 << i, ring - (1 << i)):
            pl.semaphore_signal(
                known.at[i], inc=1, device_id=device(xy, turn(z + step), core), device_id_type=MESH
            )

    rounds = log2(ring) - 1
    loads = [
        pltpu.make_async_copy(src, dst, load_sem.at[i])
        for i, (src, dst) in enumerate(
            [(tok_hbm, tok.at[core]), (og_hbm, og.at[core]), (sp_hbm, sp), (w1_hbm.at[0], w1), (w2_hbm.at[0], w2)]
        )
    ]
    for load in loads:
        load.start()

    place = lax.broadcasted_iota(jnp.int32, (slots, slots), 0)
    zl2_n = pairs // 2
    of_place = (
        (place >> log2(pairs * ny)) * (2 * ny * zl2_n)
        + ((place >> log2(zl2_n)) & 1) * (ny * zl2_n)
        + ((place >> log2(pairs)) & (ny - 1)) * zl2_n
        + (place & (zl2_n - 1))
    )
    across = lax.broadcasted_iota(jnp.int32, (slots, slots), 1)
    slot_order = (across == of_place).astype(F32).astype(BF16)
    cells = 2 * slots
    first_at = lax.broadcasted_iota(jnp.int32, (cells, cells), 0)
    second_at = lax.broadcasted_iota(jnp.int32, (cells, cells), 1)

    def by_source(at):
        kind = (at >> log2(plane)) & 1
        return (at & (plane - 1)) * (2 * pairs) + kind * pairs + (at >> log2(2 * plane))

    to_pairs = (second_at == by_source(first_at)).astype(F32).astype(BF16)
    to_sources = (first_at == by_source(second_at)).astype(F32).astype(BF16)
    pg_send[...] = jnp.zeros_like(pg_send)
    loads[2].wait()
    spt[...] = dot(slot_order, sp[...], 1, 1).astype(BF16)
    loads[0].wait()
    loads[1].wait()

    pl.semaphore_wait(barrier, plane + 2 * near)
    tell(near - 1)
    send(tok.at[core], tok.at[core], swap_s.at[0], swap_r.at[0], partner)
    send(og.at[core], og.at[core], swap_s.at[1], swap_r.at[1], partner)
    arrived(tok.at[other], swap_r.at[0])

    tok_all = tok[...].reshape(image, width)
    logits = dot(spt[...], tok_all, 1, 1)
    col_exp = jnp.exp(logits - jnp.max(logits, axis=1, keepdims=True))
    dispatch = col_exp / jnp.sum(col_exp, axis=1, keepdims=True)
    disp[...] = dispatch
    disp_b[...] = dispatch.astype(BF16)
    slot_in = dot(disp_b[...], tok[:, :, own_cols].reshape(image, half), 1, 0)
    row_exp = jnp.exp(logits - jnp.max(logits, axis=0, keepdims=True))
    combine = row_exp / jnp.sum(row_exp, axis=0, keepdims=True)
    comb[...] = combine
    arrived(og.at[other], swap_r.at[1])
    slot_grad = dot(combine.astype(BF16), og[:, :, own_cols].reshape(image, half), 1, 0)
    s_buf[...] = jnp.concatenate(
        [slot_in.reshape(plane, pairs, half), slot_grad.reshape(plane, pairs, half)], axis=1
    ).astype(BF16)

    for j in range(1, plane):
        to = shift(j)
        send(s_buf.at[to], r_buf.at[xy], p1_s.at[j], p1_r.at[xy], device(to, z, core))
    r_buf[xy] = s_buf[xy]
    for i in range(near, rounds):
        pl.semaphore_wait(known.at[i - 1], 2)
        tell(i)
    for j in range(1, plane):
        arrived(r_buf.at[shift(j)], p1_r.at[shift(j)])
    t_buf[...] = dot(to_pairs, r_buf[...].reshape(cells, half), 1, 0).astype(BF16).reshape(
        pairs, 2, plane, half
    )
    pl.semaphore_wait(known.at[rounds - 1], 2)

    hops = [(sign, d) for d in range(1, pairs, 2)] + [(-sign, d) for d in range(2, pairs, 2)]
    hops.sort(key=lambda hop: -hop[1])
    for way, d in hops:
        to = turn(z + way * d)
        send(
            t_buf.at[lax.div(to, 2)], x_buf.at[core, :, 2 * d], p2_s.at[d], p2_r.at[2 * d],
            device(xy, to, core),
        )
    mine = t_buf.at[pair]
    send(mine, x_buf.at[core, :, 1], p2_s.at[0], p2_r.at[1], sibling)
    send(mine, x_buf.at[core, :, 0], dd_s.at[0], dd_r.at[0], partner)
    x_buf[core, :, 0] = t_buf[pair]
    images = ring * plane
    hidden = w1.shape[0]

    def take(at):
        slot = x_buf.at[core, :, at]
        arrived(slot, p2_r.at[at])
        if at > 1 and at % 2 == 0:
            send(slot, x_buf.at[core, :, at + 1], rl_s.at[at // 2], p2_r.at[at + 1], sibling)
        send(slot, slot, dd_s.at[at], dd_r.at[at], partner)

    def take_first(low, high):
        for j in range(high - 1, max(low, 1) - 1, -1):
            take(2 * j)

    def take_relayed(low, high):
        for j in range(high - 1, low - 1, -1):
            take(2 * j + 1)
        for at in range(2 * low, 2 * high):
            arrived(x_buf.at[other, :, at], dd_r.at[at])

    def expert(low, high):
        count = (high - low) * 2 * plane
        span = slice(2 * low, 2 * high)

        def both(kind, weights, at, n):
            return sum(
                dot(x_buf[h, kind, span].reshape(count, half), weights[at : at + n, h * half : (h + 1) * half], 1, 1)
                for h in range(2)
            )

        for at, n in tiles(hidden):
            gelu_value, gelu_slope = gelu_parts(both(0, w1, at, n))
            gv[:count, at : at + n] = gelu_value.astype(BF16)
            pgd[:count, at : at + n] = (both(1, w2, at, n) * gelu_slope).astype(BF16)

        def product(kind, whose, at, n):
            left, right = ((gv, w2), (pgd, w1))[kind]
            cols = pl.ds(pl.multiple_of(whose * half + at, 128), n)
            return dot(left[:count], right[:, cols], 1, 0).reshape(2 * (high - low), plane, n)

        for kind in range(2):
            for at, n in tiles(half):
                o_send[kind, span, :, at : at + n] = product(kind, other, at, n).astype(BF16)
        send(o_send.at[:, span], o_recv.at[:, span], o_s.at[low], o_r.at[low], partner)
        for kind in range(2):
            for at, n in tiles(half):
                p_buf[kind, span, :, at : at + n] = product(kind, core, at, n)

    def give(low, high):
        span = slice(2 * low, 2 * high)
        arrived(o_recv.at[:, span], o_r.at[low])
        for j in range(high - 1, low - 1, -1):
            at = 2 * j + 1
            u_buf[j] = (p_buf[:, at] + o_recv[:, at].astype(F32)).astype(BF16)
            send(u_buf.at[j], v_buf.at[j], v_s.at[j], v_r.at[j], sibling)

    def pass_back(low, high):
        for j in range(high - 1, low - 1, -1):
            arrived(v_buf.at[j], v_r.at[j])
            at = 2 * j
            whole = (p_buf[:, at] + o_recv[:, at].astype(F32) + v_buf[j].astype(F32)).astype(BF16)
            if j == 0:
                b_buf[pair] = whole
            else:
                q_buf[j] = whole
                send(q_buf.at[j], b_buf.at[pair], b_s.at[j], b_r.at[pair], device(xy, turn(z + sign * j), core))

    groups = [(low, min(high, pairs)) for low, high in GROUPS if low < pairs]
    take_first(*groups[0])
    for i, group in enumerate(groups):
        if LOOK and i + 1 < len(groups):
            take_first(*groups[i + 1])
        take_relayed(*group)
        if i == 0:
            loads[3].wait()
            loads[4].wait()
        expert(*group)
        if not LOOK and i + 1 < len(groups):
            take_first(*groups[i + 1])
        give(*group)
    for group in groups:
        pass_back(*group)

    for at, n in tiles(width, 128):
        tokt[at : at + n] = tok[:, :, at : at + n].reshape(image, n).astype(F32).T.astype(BF16)

    for j in range(1, pairs):
        src = lax.rem(pair + j, pairs)
        arrived(b_buf.at[src], b_r.at[src])
    c_buf[...] = dot(to_sources, b_buf[...].reshape(cells, half), 1, 0).astype(BF16).reshape(
        plane, 2 * pairs, half
    )

    for j in range(1, plane):
        to = shift(j)
        send(c_buf.at[to], g_buf.at[xy], g_s.at[j], g_r.at[xy], device(to, z, core))
    g_buf[xy] = c_buf[xy]
    for j in range(1, plane):
        src = shift(plane - j)
        arrived(g_buf.at[src], g_r.at[src])
    came = g_buf[...].astype(F32)
    for kind in (1, 0):
        back_buf[kind, core] = came[:, kind * pairs : (kind + 1) * pairs].reshape(slots, half).astype(BF16)
        mine = back_buf.at[kind, core]
        send(mine, mine, gd_s.at[kind], gd_r.at[kind], partner)

    def inner(kind, against):
        arrived(back_buf.at[kind, other], gd_r.at[kind])
        return sum(
            dot(back_buf[kind, h], against[:, :, h * half : (h + 1) * half].reshape(image, half), 1, 1)
            for h in range(2)
        )

    disp_grad = inner(1, tok)
    comb_grad = inner(0, og)
    combine = comb[...]
    dispatch = disp[...]
    comb_inner = jnp.sum(combine * comb_grad, axis=0, keepdims=True)
    logit_grad = combine * (comb_grad - comb_inner) + dispatch * (disp_grad - jnp.sum(dispatch * disp_grad, axis=1, keepdims=True))
    lg_b[...] = logit_grad.astype(BF16)

    in_order = dot(lg_b[...], slot_order, 0, 0).astype(BF16)
    block = width // (2 * plane)
    for x_to in range(nx):
        strip_at = pl.ds(pl.multiple_of(x_to * 2 * ny * block + core * ny * block, 16), ny * block)
        pg_send[x_to * ny : (x_to + 1) * ny, :block] = (
            dot(tokt[strip_at, :], in_order, 1, 0).reshape(ny, block, slots).astype(BF16)
        )
    for j in range(1, plane):
        to = shift(j)
        send(pg_send.at[to], pg_recv.at[xy], f1_s.at[j], f1_r.at[xy], device(to, z, core))

    own_rows = pl.ds(pl.multiple_of(core * rows, rows), rows)
    for h in range(2):
        cols = slice(h * half, (h + 1) * half)
        tg[:, cols] = (
            dot(disp_b[:, own_rows], back_buf[1, h], 0, 0) + dot(lg_b[:, own_rows], spt[:, cols], 0, 0)
        ).astype(BF16)
    tg_out = pltpu.make_async_copy(tg, tg_ref, load_sem.at[5])
    tg_out.start()

    total = pg_send[xy].astype(F32)
    for j in range(1, plane):
        src = shift(plane - j)
        arrived(pg_recv.at[src], f1_r.at[src])
        total = total + pg_recv[src].astype(F32)
    pad[...] = jnp.zeros_like(pad)
    pad[:block, :slots] = total[:block]
    per = slots // ring
    f2_send[...] = pad[...].T[:slots].reshape(ring, per, pad.shape[0])

    for j in sorted(range(1, ring), key=lambda j: -min(j, ring - j)):
        to = turn(at_ex + j)
        send(
            f2_send.at[to], f2_recv.at[z], f2_s.at[j], f2_r.at[z],
            device(xy, core * zl_n + lax.div(to, 2), lax.rem(to, 2)),
        )
    stays = zh == core

    def away(start):
        copy = pltpu.make_async_remote_copy(
            src_ref=f2_send.at[at_ex], dst_ref=f2_recv.at[z], send_sem=f2_s.at[0], recv_sem=f2_r.at[z],
            device_id=device(xy, core * zl_n + zl, core), device_id_type=MESH,
        )
        if start:
            copy.start()
        else:
            copy.wait_send()

    @pl.when(stays)
    def _():
        f2_recv[z] = f2_send[at_ex]

    @pl.when(jnp.logical_not(stays))
    def _():
        away(True)
        arrived(f2_recv.at[z], f2_r.at[z])

    for j in range(1, ring):
        src = turn(z + j)
        arrived(f2_recv.at[src], f2_r.at[src])
    pg_ref[...] = jnp.sum(f2_recv[...], axis=0)[:, :block].astype(BF16)

    @pl.when(jnp.logical_not(stays))
    def _():
        away(False)

    tg_out.wait()
    for copy in started:
        copy.wait_send()


def shards(ny, tokens, out_grad, slot_param, w_in, w_out):
    dp, ex = lax.axis_size("dp"), lax.axis_size("expert")
    nx, zl_n = dp // (2 * ny), ex // 2
    plane, ring, pairs = nx * ny, 2 * zl_n, zl_n
    rows, width = tokens.shape
    slots = slot_param.shape[1]
    hidden = w_in.shape[1]
    half, image, images = width // 2, 2 * rows, ring * plane
    block, per = width // dp, slots // ex
    side = max(128, slots)
    dma = pltpu.SemaphoreType.DMA
    vmem = pltpu.VMEM
    token_grad, param_grad = pl.pallas_call(
        functools.partial(kernel, nx, ny, zl_n),
        out_shape=(
            jax.ShapeDtypeStruct((rows, width), BF16),
            jax.ShapeDtypeStruct((per, block), BF16),
        ),
        in_specs=[pl.BlockSpec(memory_space=pl.ANY)] * 5,
        out_specs=(pl.BlockSpec(memory_space=pl.ANY), pl.BlockSpec(memory_space=pltpu.VMEM)),
        scratch_shapes=[
            vmem((2, rows, width), BF16),
            vmem((2, rows, width), BF16),
            vmem((width, slots), BF16),
            vmem((hidden, width), BF16),
            vmem((hidden, width), BF16),
            vmem((slots, width), BF16),
            vmem((width, image), BF16),
            vmem((slots, image), F32),
            vmem((slots, image), F32),
            vmem((slots, image), BF16),
            vmem((slots, image), BF16),
            vmem((plane, 2 * pairs, half), BF16),
            vmem((plane, 2 * pairs, half), BF16),
            vmem((pairs, 2, plane, half), BF16),
            vmem((2, 2, ring, plane, half), BF16),
            vmem((images, hidden), BF16),
            vmem((images, hidden), BF16),
            vmem((2, ring, plane, half), F32),
            vmem((2, ring, plane, half), BF16),
            vmem((2, ring, plane, half), BF16),
            vmem((pairs, 2, plane, half), BF16),
            vmem((pairs, 2, plane, half), BF16),
            vmem((pairs, 2, plane, half), BF16),
            vmem((pairs, 2, plane, half), BF16),
            vmem((plane, 2 * pairs, half), BF16),
            vmem((plane, 2 * pairs, half), BF16),
            vmem((2, 2, slots, half), BF16),
            vmem((plane, up16(block), slots), BF16),
            vmem((plane, up16(block), slots), BF16),
            vmem((side, side), F32),
            vmem((ring, per, side), F32),
            vmem((ring, per, side), F32),
            dma((6,)),
            dma((2,)), dma((2,)),
            dma((plane,)), dma((plane,)),
            dma((pairs,)), dma((ring,)), dma((pairs,)),
            dma((ring,)), dma((ring,)),
            dma((pairs,)), dma((pairs,)),
            dma((pairs,)), dma((pairs,)),
            dma((pairs,)), dma((pairs,)),
            dma((plane,)), dma((plane,)),
            dma((2,)), dma((2,)),
            dma((plane,)), dma((plane,)),
            dma((ring,)), dma((ring,)),
            pltpu.SemaphoreType.REGULAR((max(1, ring.bit_length() - 2),)),
            vmem((rows, width), BF16),
        ],
        compiler_params=pltpu.CompilerParams(
            collective_id=0, has_side_effects=True, vmem_limit_bytes=60 << 20
        ),
    )(tokens, out_grad, slot_param, w_in, w_out)
    return token_grad, param_grad.T


def solution(mesh):
    placed = (
        P(("dp", "expert"), None),
        P(("dp", "expert"), None),
        P(),
        P(("dp", "expert"), None, None),
        P(("dp", "expert"), None, None),
    )
    return jax.shard_map(
        functools.partial(shards, PLANE_Y),
        mesh=mesh,
        in_specs=placed,
        out_specs=(P(("dp", "expert"), None), P("dp", "expert")),
        check_vma=False,
    )
```
